32 devices in a mesh: group: 2 (over y), ep: 4 (over z), tp: 4 (over x, core).
Axes of the slice: x: 2, y: 2, z: 4, core: 2. Of those that a mesh axis runs over, the one named last changes fastest.
Arguments:
- tokens: bfloat16 [512, 3584], P(('group', 'ep'), 'tp'), parts along dimension 0, may hold values from -6 to 6
- routes: int32 [512, 2], P(('group', 'ep')), parts along dimension 0, may hold values from 0 to 3, all different within a row; in each aligned block of 64 rows (0 to 63, 64 to 127, ...) at most 64 rows name the same one
- scores: float32 [512, 2], P(('group', 'ep')), parts along dimension 0, may hold values from 0.05 to 1
- w_up: bfloat16 [4, 3584, 1024], P('ep', 'tp'), may hold values from -0.09375 to 0.09375
- w_down: bfloat16 [4, 1024, 3584], P('ep', None, 'tp'), may hold values from -0.1875 to 0.1875
Outputs:
- mixed: bfloat16 [512, 3584], P(('group', 'ep'), 'tp'), parts along dimension 0
The draws below stay inside these ranges and needn't reach their ends.
There are 2 independent parts, one for each index of `group`. The reference program is written for one: setup_inputs(seed, part) draws one part's arguments, and reference() takes and returns one part's arrays. A program takes and returns all parts, laid end to end along the dimension named above; an argument that names none is the same for every part. Nothing has to cross between parts.
Inputs may be any that keep to these rules, and one draw needn't show every extreme that they name: `routes`: within the rows of one index of ep, each expert is named at most 64 times, and no row names an expert twice.
All inputs are finite; a program needn't handle non-finite values.
Results may differ from the reference program's by a relative error of at most 0.015.
Values may be sent and summed in bfloat16 or wider, within the bound.
A program may use at most 64 MiB of HBM per device.

```python
import math
import jax
import jax.numpy as jnp
import numpy as np
from jax import lax

D = 3584
H = 1024
TOK_DEV = 64
TOP = 2
EXPERTS = 4
CAP = 64
TOKENS = 256
N_EP = 4
N_TP = 4


def block_levels(own_key, dims, shards, low, top_value):
    level, own = 1.0, jax.random.fold_in(own_key, 6)
    for dim, shards_of in shards:
        steps = jnp.exp(jax.random.uniform(jax.random.fold_in(own, dim), (shards_of,), jnp.float32, low / len(shards), top_value / len(shards)))
        level = level * jnp.repeat(steps, dims[dim] // shards_of).reshape([-1 if axis == dim else 1 for axis in range(len(dims))])
    return level


def routed_block(rng, own, number, rows, number_of, top, reach, lean):
    ranking = jax.random.permutation(rng, number_of)
    heavy_load, ordinary = portions_of(number_of, rows * top, reach, lean, True), portions_of(number_of, rows * top, reach, lean, False)
    places = jnp.arange(number_of)

    def named(lengths, turn):
        used = int((lengths > 0).sum())
        fixed = max(1, used // 4)
        moved = fixed + (places - fixed + turn * (used - fixed)) % max(1, number_of - fixed)
        return jnp.zeros((number_of,), jnp.int32).at[ranking[jnp.where(places < fixed, places, moved)]].set(jnp.asarray(lengths, jnp.int32))

    lengths = jnp.where(number % 4 == 0, named(heavy_load, number // 4), named(ordinary, number - number // 4 - 1))
    mixed = jax.random.permutation(jax.random.fold_in(own, 3), number_of)
    donor, receiver = mixed[0:number_of // 2 * 2:2], mixed[1:number_of // 2 * 2:2]
    slack = jnp.minimum(lengths[donor] - 1, reach - lengths[receiver]) // 2
    slack = jnp.where((donor == ranking[0]) | (receiver == ranking[0]) | (lengths[receiver] == 0), 0, jnp.maximum(slack, 0))
    moved = jax.random.randint(jax.random.fold_in(own, 4), (number_of // 2,), 0, 1 << 20) % (slack + 1)
    lengths = lengths.at[donor].add(-moved).at[receiver].add(moved)
    items = jnp.searchsorted(jnp.cumsum(lengths), jnp.arange(rows * top), side="right").astype(jnp.int32)
    grid = items.reshape(top, rows).T
    grid = grid[jax.random.permutation(jax.random.fold_in(own, 1), rows)]
    turn = jax.random.randint(jax.random.fold_in(own, 2), (rows, 1), 0, top)
    return jnp.take_along_axis(grid, (jnp.arange(top)[None, :] + turn) % top, axis=1)


def portions_of(number_of, total, most, skew, full):
    weights = [(1 << 20) // math.isqrt(standing ** skew) + 1 for standing in range(1, number_of + 1)]
    largest = most if full else min(most, max(-(-total // number_of), total * weights[0] // sum(weights)))
    least = 1 if total - largest >= number_of - 1 else 0
    holding, spare = [largest] + [least] * (number_of - 1), total - largest - least * (number_of - 1)
    while spare > 0:
        movable = [i for i in range(1, number_of) if holding[i] < largest] or [i for i in range(1, number_of) if holding[i] < most]
        pool, left = sum([weights[i] for i in movable]), spare
        for i in movable:
            extra = min(most - holding[i], max(1, left * weights[i] // pool), spare)
            holding[i] = holding[i] + extra
            spare = spare - extra
    return np.array(holding)


def bell_draw(stream_key, dims, width, limit, shards=(), kind=jnp.bfloat16):
    array = jax.random.normal(stream_key, dims, jnp.float32) * width
    if len(shards) > 0:
        array = block_levels(stream_key, dims, shards, -0.22, 0.18) * array
    return jnp.clip(array, min=-limit, max=limit).astype(kind)


def setup_inputs(seed: int = 0, part: int = 0) -> dict:
    key_list = jax.random.split(jax.random.key(seed), 6)
    part_splits = jax.random.split(jax.random.fold_in(key_list[5], part), 6)
    tokens = bell_draw(part_splits[0], (TOKENS, D), 1.0, 6.0, ((0, 4), (1, 4)))
    routes_keys = jax.random.split(jax.random.fold_in(part_splits[1], 1), TOKENS // TOK_DEV)
    routes_turns = jax.random.permutation(jax.random.fold_in(part_splits[1], 3), TOKENS // TOK_DEV)
    routes = jax.vmap(lambda own, number: routed_block(jax.random.fold_in(part_splits[1], 2), own, number, TOK_DEV, EXPERTS, TOP, CAP, 2))(routes_keys, routes_turns).reshape((TOKENS, TOP))
    scores = jnp.clip(jnp.exp(math.log(1.0) - 2.9957323 * jax.random.uniform(part_splits[2], (TOKENS, TOP), jnp.float32) ** block_levels(part_splits[2], (TOKENS, TOP), ((0, 4),), -0.2, 0.2)), 0.05, 1.0)
    w_up = bell_draw(key_list[3], (EXPERTS, D, H), D ** -0.5, 0.09375, ((0, 4), (1, 4)))
    w_down = bell_draw(key_list[4], (EXPERTS, H, D), H ** -0.5, 0.1875, ((0, 4), (2, 4)))
    return dict(tokens=tokens, routes=routes, scores=scores, w_up=w_up, w_down=w_down)


SCALE = 2.5


def reference(tokens, routes, scores, w_up, w_down):
    capacity = 2 * TOK_DEV * TOP // N_EP
    block_ids = routes.reshape(N_EP, TOK_DEV * TOP)
    onehot = (block_ids[:, :, None] == jnp.arange(EXPERTS, dtype=jnp.int32)[None, None, :]).astype(jnp.int32)
    slot_rank = jnp.sum((jnp.cumsum(onehot, axis=1) - onehot) * onehot, axis=2)
    sender = jnp.arange(N_EP, dtype=jnp.int32)[:, None]
    slot_index = ((block_ids * N_EP + sender) * capacity + slot_rank).reshape(-1).astype(jnp.int32)
    pair_token = (jnp.arange(TOKENS * TOP, dtype=jnp.int32) // TOP).astype(jnp.int32)
    slot_total = EXPERTS * N_EP * capacity
    source_ids = jnp.full((slot_total,), -1, jnp.int32).at[slot_index].set(pair_token)
    source_ids = source_ids.reshape(EXPERTS, N_EP * capacity)
    block_width = D // N_TP

    def expert(packed):
        chosen, up_matrix, down_matrix = packed
        row_data = tokens[jnp.maximum(chosen, 0)]
        row_data = jnp.where((chosen >= 0)[:, None], row_data, jnp.zeros_like(row_data))
        pre_act = jnp.zeros((row_data.shape[0], H), jnp.float32)
        for block in range(N_TP):
            lower = block * block_width
            part_sum = jnp.dot(row_data[:, lower:lower + block_width], up_matrix[lower:lower + block_width, :], preferred_element_type=jnp.float32)
            rounded = lax.optimization_barrier(part_sum.astype(jnp.bfloat16))
            pre_act = pre_act + rounded.astype(jnp.float32)
        hidden = jax.nn.silu(pre_act).astype(jnp.bfloat16)
        return jnp.dot(hidden, down_matrix, preferred_element_type=jnp.float32).astype(jnp.bfloat16)

    expert_rows = lax.map(expert, (source_ids, w_up, w_down)).reshape(slot_total, D)
    weights = SCALE * scores / jnp.sum(scores, axis=1, keepdims=True)
    slot_of_pair = slot_index.reshape(TOKENS, TOP)
    total = jnp.zeros((TOKENS, D), jnp.float32)
    for column in range(TOP):
        picked = expert_rows[slot_of_pair[:, column]].astype(jnp.float32)
        total = total + weights[:, column:column + 1] * picked
    return total.astype(jnp.bfloat16)
```

```python
import functools

import jax
import jax.numpy as jnp
from jax import lax
from jax.experimental import pallas as pl
from jax.experimental.pallas import tpu as pltpu
from jax.sharding import PartitionSpec as P

SCALE = 2.5
MESH = pl.DeviceIdType.MESH
N = 4


def partner(e, k):
    return (e, e + 1 - 2 * lax.rem(e, 2), lax.rem(e + 2, N), N - 1 - e)[k]


def kernel(
    tok_hbm, routes_ref, scores_ref, up_hbm, down_hbm, out_ref,
    up, down, arrived, part, from_core, from_chip, pair_sum, outgoing, hidden, result, returned,
    load_sem, a_send, a_recv, core_send, core_recv, chip_send, chip_recv, hid_send, hid_recv, c_send, c_recv,
):
    e = lax.axis_index("ep")
    tp = lax.axis_index("tp")
    core = lax.rem(tp, 2)
    other = 1 - core
    sibling = {"tp": tp + 1 - 2 * core}
    across = {"tp": lax.rem(tp + 2, N)}
    rows = out_ref.shape[0]

    load_tok = pltpu.make_async_copy(tok_hbm, arrived.at[0], load_sem.at[0])
    load_up = pltpu.make_async_copy(up_hbm.at[0], up, load_sem.at[1])
    load_down = pltpu.make_async_copy(down_hbm.at[0], down, load_sem.at[2])
    load_tok.start()
    load_up.start()
    load_down.start()

    barrier = pltpu.get_barrier_semaphore()
    for k in range(1, N):
        pl.semaphore_signal(barrier, inc=1, device_id={"ep": partner(e, k)}, device_id_type=MESH)
    pl.semaphore_signal(barrier, inc=1, device_id=sibling, device_id_type=MESH)
    pl.semaphore_signal(barrier, inc=1, device_id=across, device_id_type=MESH)
    pl.semaphore_wait(barrier, N + 1)

    def remote(src, dst, send, recv, k, device):
        return pltpu.make_async_remote_copy(
            src_ref=src, dst_ref=dst, send_sem=send.at[k], recv_sem=recv.at[k],
            device_id=device, device_id_type=MESH,
        )

    def a_copy(k):
        return remote(tok_hbm, arrived.at[k], a_send, a_recv, k, {"ep": partner(e, k)})

    def core_copy(k):
        return remote(part.at[k, other], from_core.at[k], core_send, core_recv, k, sibling)

    def chip_copy(k):
        return remote(outgoing.at[k], from_chip.at[k], chip_send, chip_recv, k, across)

    def hid_copy(k):
        return remote(hidden.at[k, core], hidden.at[k, core], hid_send, hid_recv, k, sibling)

    def c_copy(k):
        return remote(result.at[k], returned.at[k], c_send, c_recv, k, {"ep": partner(e, k)})

    for k in range(1, N):
        a_copy(k).start()

    half = rows // 2

    scores = scores_ref[...]
    weights = SCALE * scores / jnp.sum(scores, axis=0, keepdims=True)
    routes = routes_ref[...]
    square = (rows, rows)
    diagonal = lax.broadcasted_iota(jnp.int32, square, 0) == lax.broadcasted_iota(jnp.int32, square, 1)
    factors = []
    for k in range(N):
        row = jnp.sum(jnp.where(routes == partner(e, k), weights, 0.0), axis=0, keepdims=True)
        factors.append(jnp.sum(jnp.where(diagonal, row, 0.0), axis=1, keepdims=True))

    def up_stage(k):
        if k == 0:
            load_tok.wait()
            load_up.wait()
        else:
            a_copy(k).wait_recv()
        value = jnp.dot(arrived[k], up[...], preferred_element_type=jnp.float32).astype(jnp.bfloat16)
        part[k] = value.reshape(2, half, value.shape[1])
        core_copy(k).start()

    def chip_stage(k):
        core_copy(k).wait_recv()
        both = part[k, core].astype(jnp.float32) + from_core[k].astype(jnp.float32)
        pair_sum[k] = both
        outgoing[k] = both.astype(jnp.bfloat16)
        chip_copy(k).start()

    def hidden_stage(k):
        chip_copy(k).wait_recv()
        value = pair_sum[k] + from_chip[k].astype(jnp.float32)
        hidden[k, core] = (value / (1.0 + jnp.exp(-value))).astype(jnp.bfloat16)
        hid_copy(k).start()

    def down_stage(k):
        hid_copy(k).wait_recv()
        if k == 0:
            load_down.wait()
        rows_in = hidden[k].reshape(rows, hidden.shape[3])
        value = jnp.dot(rows_in, down[...], preferred_element_type=jnp.float32).astype(jnp.bfloat16)
        if k == 0:
            returned[0] = value
        else:
            result[k] = value
            c_copy(k).start()

    order = (0, 1, 3, 2)
    for t in range(N + 3):
        for lag, stage in ((3, down_stage), (2, hidden_stage), (1, chip_stage), (0, up_stage)):
            if 0 <= t - lag < N:
                stage(order[t - lag])

    mixed = jnp.zeros(out_ref.shape, jnp.float32)
    for k in order:
        if k > 0:
            c_copy(k).wait_recv()
        mixed = mixed + factors[k] * returned[k].astype(jnp.float32)
    out_ref[...] = mixed.astype(out_ref.dtype)

    for k in range(N):
        core_copy(k).wait_send()
        chip_copy(k).wait_send()
        hid_copy(k).wait_send()
        if k > 0:
            a_copy(k).wait_send()
            c_copy(k).wait_send()


def dense_body(tokens, routes, scores, w_up, w_down):
    rows, quarter = tokens.shape
    width = w_up.shape[2]
    half = rows // 2
    bf16, f32 = jnp.bfloat16, jnp.float32
    vmem = pl.BlockSpec(memory_space=pltpu.VMEM)
    anywhere = pl.BlockSpec(memory_space=pl.ANY)
    dma = pltpu.SemaphoreType.DMA
    return pl.pallas_call(
        kernel,
        out_shape=jax.ShapeDtypeStruct((rows, quarter), bf16),
        in_specs=[anywhere, vmem, vmem, anywhere, anywhere],
        out_specs=vmem,
        scratch_shapes=[
            pltpu.VMEM((quarter, width), bf16),
            pltpu.VMEM((width, quarter), bf16),
            pltpu.VMEM((N, rows, quarter), bf16),
            pltpu.VMEM((N, 2, half, width), bf16),
            pltpu.VMEM((N, half, width), bf16),
            pltpu.VMEM((N, half, width), bf16),
            pltpu.VMEM((N, half, width), f32),
            pltpu.VMEM((N, half, width), bf16),
            pltpu.VMEM((N, 2, half, width), bf16),
            pltpu.VMEM((N, rows, quarter), bf16),
            pltpu.VMEM((N, rows, quarter), bf16),
            dma((3,)),
        ] + [dma((N,))] * 10,
        compiler_params=pltpu.CompilerParams(
            collective_id=0, has_side_effects=True, vmem_limit_bytes=60 * 1024 * 1024
        ),
        cost_estimate=pl.CostEstimate(
            flops=4 * N * rows * quarter * width, bytes_accessed=4 * quarter * width, transcendentals=N * rows * width
        ),
        name="expert_layer",
    )(tokens, routes.T, scores.T, w_up, w_down)


def body(tokens, routes, scores, w_up, w_down):
    rows_here, quarter = tokens.shape
    chosen = routes.shape[1]
    owners = lax.axis_size("ep")
    capacity = 2 * rows_here * chosen // owners
    flat_ids = routes.reshape(-1)
    onehot = (flat_ids[:, None] == jnp.arange(owners, dtype=jnp.int32)[None, :]).astype(jnp.int32)
    slot_rank = jnp.sum((jnp.cumsum(onehot, axis=0) - onehot) * onehot, axis=1)
    target = flat_ids * capacity + slot_rank
    pair_token = jnp.arange(rows_here * chosen, dtype=jnp.int32) // chosen
    matches = target[None, :] == jnp.arange(owners * capacity, dtype=jnp.int32)[:, None]
    source = jnp.sum(jnp.where(matches, pair_token[None, :] + 1, 0), axis=1) - 1
    picked = jnp.take(tokens, jnp.maximum(source, 0), axis=0)
    outgoing = jnp.where((source >= 0)[:, None], picked, jnp.zeros_like(picked)).reshape(
        owners, capacity, quarter
    )
    up_local = w_up[0]
    down_local = w_down[0]
    arrived = lax.all_to_all(outgoing, "ep", split_axis=0, concat_axis=0, tiled=True)
    senders, slot_count, columns = arrived.shape
    flat_rows = arrived.reshape(senders * slot_count, columns)
    partial_value = jnp.dot(flat_rows, up_local, preferred_element_type=jnp.float32)
    hidden = jax.nn.silu(
        lax.psum(partial_value.astype(jnp.bfloat16), "tp").astype(jnp.float32)
    ).astype(jnp.bfloat16)
    result = jnp.dot(hidden, down_local, preferred_element_type=jnp.float32).astype(jnp.bfloat16)
    returned_rows = lax.all_to_all(
        result.reshape(senders, slot_count, columns), "ep", split_axis=0, concat_axis=0, tiled=True
    )
    back_flat = returned_rows.reshape(owners * capacity, quarter)
    gathered = (
        jnp.take(back_flat, target, axis=0).reshape(rows_here, chosen, quarter).astype(jnp.float32)
    )
    weights = SCALE * scores / jnp.sum(scores, axis=1, keepdims=True)
    mixed = jnp.einsum("tk,tkd->td", weights, gathered, precision=lax.Precision.HIGHEST)
    return mixed.astype(jnp.bfloat16)


def solution(mesh):
    in_specs = (
        P(("group", "ep"), "tp"),
        P(("group", "ep"), None),
        P(("group", "ep"), None),
        P("ep", "tp", None),
        P("ep", None, "tp"),
    )
    out_specs = P(("group", "ep"), "tp")
    shape = mesh.shape
    small = shape["ep"] == N and shape["tp"] == N
    return jax.shard_map(dense_body if small else body, mesh=mesh, in_specs=in_specs, out_specs=out_specs, check_vma=False)
```

```python
import functools

import jax
import jax.numpy as jnp
from jax import lax
from jax.experimental import pallas as pl
from jax.experimental.pallas import tpu as pltpu
from jax.sharding import PartitionSpec as P

SCALE = 2.5
MESH = pl.DeviceIdType.MESH
N = 4


SCHEDULE = (
    "u0 c0 S2 u1 "
    "F c1 S3 h0 "
    "d0 u2 c2 u3 "
    "c3 h1 d1 h2 "
    "d2 h3 d3 "
)


def partners(e):
    middle = lax.rem((e + 1) // 2, 2)
    slots = (0, 1, 2 + middle, 3 - middle)
    near = e + 1 - 2 * lax.rem(e, 2)
    cross, flip = lax.rem(e + 2, N), N - 1 - e
    second = middle * flip + (1 - middle) * cross
    third = middle * cross + (1 - middle) * flip
    return middle, slots, (e, near, second, third)


def kernel(
    tok_hbm, routes_ref, scores_ref, up_hbm, down_hbm, out_ref,
    up, down, arrived, part, from_core, from_chip, pair_sum, outgoing, hidden, result, returned,
    load_sem, a_send, a_recv, core_send, core_recv, chip_send, chip_recv, hid_send, hid_recv, c_send, c_recv, far_sem,
):
    e = lax.axis_index("ep")
    tp = lax.axis_index("tp")
    middle, slots, peers = partners(e)
    core = lax.rem(tp, 2)
    other = 1 - core
    sibling = {"tp": tp + 1 - 2 * core}
    across = {"tp": lax.rem(tp + 2, N)}
    rows = out_ref.shape[0]

    load_tok = pltpu.make_async_copy(tok_hbm, arrived.at[0], load_sem.at[0])
    load_up = pltpu.make_async_copy(up_hbm.at[0], up, load_sem.at[1])
    load_down = pltpu.make_async_copy(down_hbm.at[0], down, load_sem.at[2])
    load_tok.start()
    load_up.start()
    load_down.start()

    barrier = pltpu.get_barrier_semaphore()
    pl.semaphore_signal(barrier, inc=1, device_id={"ep": peers[1]}, device_id_type=MESH)

    @pl.when(middle == 1)
    def _():
        pl.semaphore_signal(barrier, inc=1, device_id={"ep": peers[2]}, device_id_type=MESH)

    pl.semaphore_signal(barrier, inc=1, device_id=sibling, device_id_type=MESH)
    pl.semaphore_signal(barrier, inc=1, device_id=across, device_id_type=MESH)
    pl.semaphore_wait(barrier, 3 + middle)

    def remote(src, dst, send, recv, k, device):
        return pltpu.make_async_remote_copy(
            src_ref=src, dst_ref=dst, send_sem=send.at[k], recv_sem=recv.at[k],
            device_id=device, device_id_type=MESH,
        )

    def a_copy(k):
        return remote(tok_hbm, arrived.at[slots[k]], a_send, a_recv, slots[k], {"ep": peers[k]})

    def forward_copy():
        return remote(arrived.at[slots[2]], arrived.at[2], a_send, a_recv, 2, {"ep": peers[1]})

    def core_copy(k):
        return remote(part.at[k, other], from_core.at[k], core_send, core_recv, k, sibling)

    def chip_copy(k):
        return remote(outgoing.at[k], from_chip.at[k], chip_send, chip_recv, k, across)

    def hid_copy(k):
        return remote(hidden.at[k, core], hidden.at[k, core], hid_send, hid_recv, k, sibling)

    def c_copy(k):
        return remote(result.at[k], returned.at[slots[k]], c_send, c_recv, slots[k], {"ep": peers[k]})

    a_copy(1).start()

    @pl.when(middle == 1)
    def _():
        a_copy(2).start()
        for k in (1, 2):
            pl.semaphore_signal(far_sem.at[0], inc=1, device_id={"ep": peers[k]}, device_id_type=MESH)

    def second_sends():
        a_copy(1).wait_send()
        pl.semaphore_wait(far_sem.at[0], 1)

        @pl.when(middle == 1)
        def _():
            pl.semaphore_signal(far_sem.at[1], inc=1, device_id={"ep": peers[1]}, device_id_type=MESH)

        @pl.when(middle == 0)
        def _():
            a_copy(2).start()

    def forward():
        @pl.when(middle == 1)
        def _():
            a_copy(2).wait_recv()
            forward_copy().start()

    def third_send(after):
        @pl.when(middle == 0)
        def _():
            if after:
                a_copy(2).wait_send()
            pl.semaphore_wait(far_sem.at[1], 1)
            a_copy(3).start()

        if after:
            @pl.when(middle == 1)
            def _():
                a_copy(2).wait_send()

    half = rows // 2

    scores = scores_ref[...]
    weights = SCALE * scores / jnp.sum(scores, axis=0, keepdims=True)
    routes = routes_ref[...]
    square = (rows, rows)
    diagonal = lax.broadcasted_iota(jnp.int32, square, 0) == lax.broadcasted_iota(jnp.int32, square, 1)
    factors = []
    for k in range(N):
        row = jnp.sum(jnp.where(routes == peers[k], weights, 0.0), axis=0, keepdims=True)
        factors.append(jnp.sum(jnp.where(diagonal, row, 0.0), axis=1, keepdims=True))

    def up_stage(k):
        if k == 0:
            load_tok.wait()
            load_up.wait()
        elif k == 2:
            @pl.when(middle == 0)
            def _():
                a_copy(2).wait_recv()
        else:
            a_copy(k).wait_recv()
        value = jnp.dot(arrived[slots[k]], up[...], preferred_element_type=jnp.float32).astype(jnp.bfloat16)
        part[k] = value.reshape(2, half, value.shape[1])
        core_copy(k).start()

    def chip_stage(k):
        core_copy(k).wait_recv()
        both = part[k, core].astype(jnp.float32) + from_core[k].astype(jnp.float32)
        pair_sum[k] = both
        outgoing[k] = both.astype(jnp.bfloat16)
        chip_copy(k).start()

    def hidden_stage(k):
        chip_copy(k).wait_recv()
        value = pair_sum[k] + from_chip[k].astype(jnp.float32)
        hidden[k, core] = (value / (1.0 + jnp.exp(-value))).astype(jnp.bfloat16)
        hid_copy(k).start()

    def down_stage(k):
        hid_copy(k).wait_recv()
        if k == 0:
            load_down.wait()
        rows_in = hidden[k].reshape(rows, hidden.shape[3])
        value = jnp.dot(rows_in, down[...], preferred_element_type=jnp.float32).astype(jnp.bfloat16)
        if k == 0:
            returned[0] = value
        else:
            result[k] = value
            c_copy(k).start()

    stages = {"u": up_stage, "c": chip_stage, "h": hidden_stage, "d": down_stage}
    for step in SCHEDULE.split():
        if step == "S2":
            second_sends()
        elif step == "F":
            forward()
        elif step in ("S3", "X3"):
            third_send(step == "S3")
        else:
            stages[step[0]](int(step[1]))

    mixed = jnp.zeros(out_ref.shape, jnp.float32)
    for k in range(N):
        if k > 0:
            c_copy(k).wait_recv()
        mixed = mixed + factors[k] * returned[slots[k]].astype(jnp.float32)
    out_ref[...] = mixed.astype(out_ref.dtype)

    for k in range(N):
        core_copy(k).wait_send()
        chip_copy(k).wait_send()
        hid_copy(k).wait_send()
        if k > 0:
            if k == 3 or (k == 2 and "X3" in SCHEDULE):
                a_copy(k).wait_send()
            c_copy(k).wait_send()


def dense_body(tokens, routes, scores, w_up, w_down):
    rows, quarter = tokens.shape
    width = w_up.shape[2]
    half = rows // 2
    bf16, f32 = jnp.bfloat16, jnp.float32
    vmem = pl.BlockSpec(memory_space=pltpu.VMEM)
    anywhere = pl.BlockSpec(memory_space=pl.ANY)
    dma = pltpu.SemaphoreType.DMA
    return pl.pallas_call(
        kernel,
        out_shape=jax.ShapeDtypeStruct((rows, quarter), bf16),
        in_specs=[anywhere, vmem, vmem, anywhere, anywhere],
        out_specs=vmem,
        scratch_shapes=[
            pltpu.VMEM((quarter, width), bf16),
            pltpu.VMEM((width, quarter), bf16),
            pltpu.VMEM((N, rows, quarter), bf16),
            pltpu.VMEM((N, 2, half, width), bf16),
            pltpu.VMEM((N, half, width), bf16),
            pltpu.VMEM((N, half, width), bf16),
            pltpu.VMEM((N, half, width), f32),
            pltpu.VMEM((N, half, width), bf16),
            pltpu.VMEM((N, 2, half, width), bf16),
            pltpu.VMEM((N, rows, quarter), bf16),
            pltpu.VMEM((N, rows, quarter), bf16),
            dma((3,)),
        ] + [dma((N,))] * 10 + [pltpu.SemaphoreType.REGULAR((2,))],
        compiler_params=pltpu.CompilerParams(
            collective_id=0, has_side_effects=True, vmem_limit_bytes=60 * 1024 * 1024
        ),
        cost_estimate=pl.CostEstimate(
            flops=4 * N * rows * quarter * width, bytes_accessed=4 * quarter * width, transcendentals=N * rows * width
        ),
        name="expert_layer",
    )(tokens, routes.T, scores.T, w_up, w_down)


def body(tokens, routes, scores, w_up, w_down):
    rows_here, quarter = tokens.shape
    chosen = routes.shape[1]
    owners = lax.axis_size("ep")
    capacity = 2 * rows_here * chosen // owners
    flat_ids = routes.reshape(-1)
    onehot = (flat_ids[:, None] == jnp.arange(owners, dtype=jnp.int32)[None, :]).astype(jnp.int32)
    slot_rank = jnp.sum((jnp.cumsum(onehot, axis=0) - onehot) * onehot, axis=1)
    target = flat_ids * capacity + slot_rank
    pair_token = jnp.arange(rows_here * chosen, dtype=jnp.int32) // chosen
    matches = target[None, :] == jnp.arange(owners * capacity, dtype=jnp.int32)[:, None]
    source = jnp.sum(jnp.where(matches, pair_token[None, :] + 1, 0), axis=1) - 1
    picked = jnp.take(tokens, jnp.maximum(source, 0), axis=0)
    outgoing = jnp.where((source >= 0)[:, None], picked, jnp.zeros_like(picked)).reshape(
        owners, capacity, quarter
    )
    up_local = w_up[0]
    down_local = w_down[0]
    arrived = lax.all_to_all(outgoing, "ep", split_axis=0, concat_axis=0, tiled=True)
    senders, slot_count, columns = arrived.shape
    flat_rows = arrived.reshape(senders * slot_count, columns)
    partial_value = jnp.dot(flat_rows, up_local, preferred_element_type=jnp.float32)
    hidden = jax.nn.silu(
        lax.psum(partial_value.astype(jnp.bfloat16), "tp").astype(jnp.float32)
    ).astype(jnp.bfloat16)
    result = jnp.dot(hidden, down_local, preferred_element_type=jnp.float32).astype(jnp.bfloat16)
    returned_rows = lax.all_to_all(
        result.reshape(senders, slot_count, columns), "ep", split_axis=0, concat_axis=0, tiled=True
    )
    back_flat = returned_rows.reshape(owners * capacity, quarter)
    gathered = (
        jnp.take(back_flat, target, axis=0).reshape(rows_here, chosen, quarter).astype(jnp.float32)
    )
    weights = SCALE * scores / jnp.sum(scores, axis=1, keepdims=True)
    mixed = jnp.einsum("tk,tkd->td", weights, gathered, precision=lax.Precision.HIGHEST)
    return mixed.astype(jnp.bfloat16)


def solution(mesh):
    in_specs = (
        P(("group", "ep"), "tp"),
        P(("group", "ep"), None),
        P(("group", "ep"), None),
        P("ep", "tp", None),
        P("ep", None, "tp"),
    )
    out_specs = P(("group", "ep"), "tp")
    shape = mesh.shape
    small = shape["ep"] == N and shape["tp"] == N
    return jax.shard_map(dense_body if small else body, mesh=mesh, in_specs=in_specs, out_specs=out_specs, check_vma=False)
```

```python
import functools

import jax
import jax.numpy as jnp
from jax import lax
from jax.experimental import pallas as pl
from jax.experimental.pallas import tpu as pltpu
from jax.sharding import PartitionSpec as P

SCALE = 2.5
MESH = pl.DeviceIdType.MESH
N = 4


SCHEDULE = (
    "u0", "S2", "c0", "u1", "c1", "X3", "h0", "u2", "c2", "h1",
    "u3", "c3", "d1", "h2", "d2", "h3", "d3", "d0",
)


def partners(e):
    middle = lax.rem((e + 1) // 2, 2)
    slots = (0, 1 + 2 * middle, 2 - middle, 3 - middle)
    near = e + 1 - 2 * lax.rem(e, 2)
    cross, flip = lax.rem(e + 2, N), N - 1 - e
    first = middle * flip + (1 - middle) * near
    second = middle * near + (1 - middle) * cross
    third = middle * cross + (1 - middle) * flip
    return middle, slots, (e, first, second, third)


def kernel(
    tok_hbm, routes_ref, scores_ref, up_hbm, down_hbm, out_ref,
    up, down, arrived, part, from_core, from_chip, pair_sum, outgoing, hidden, result, returned,
    load_sem, a_send, a_recv, core_send, core_recv, chip_send, chip_recv, hid_send, hid_recv, c_send, c_recv, far_sem,
):
    e = lax.axis_index("ep")
    tp = lax.axis_index("tp")
    middle, slots, peers = partners(e)
    core = lax.rem(tp, 2)
    other = 1 - core
    sibling = {"tp": tp + 1 - 2 * core}
    across = {"tp": lax.rem(tp + 2, N)}
    rows = out_ref.shape[0]

    load_tok = pltpu.make_async_copy(tok_hbm, arrived.at[0], load_sem.at[0])
    load_up = pltpu.make_async_copy(up_hbm.at[0], up, load_sem.at[1])
    load_down = pltpu.make_async_copy(down_hbm.at[0], down, load_sem.at[2])
    load_tok.start()
    load_up.start()
    load_down.start()

    barrier = pltpu.get_barrier_semaphore()
    pl.semaphore_signal(barrier, inc=1, device_id={"ep": peers[1]}, device_id_type=MESH)

    @pl.when(middle == 1)
    def _():
        pl.semaphore_signal(barrier, inc=1, device_id={"ep": peers[2]}, device_id_type=MESH)

    pl.semaphore_signal(barrier, inc=1, device_id=sibling, device_id_type=MESH)
    pl.semaphore_signal(barrier, inc=1, device_id=across, device_id_type=MESH)
    pl.semaphore_wait(barrier, 3 + middle)

    def remote(src, dst, send, recv, k, device):
        return pltpu.make_async_remote_copy(
            src_ref=src, dst_ref=dst, send_sem=send.at[k], recv_sem=recv.at[k],
            device_id=device, device_id_type=MESH,
        )

    def a_copy(k):
        return remote(tok_hbm, arrived.at[slots[k]], a_send, a_recv, slots[k], {"ep": peers[k]})

    def forward_copy():
        return remote(arrived.at[slots[1]], arrived.at[2], a_send, a_recv, 2, {"ep": peers[2]})

    def core_copy(k):
        return remote(part.at[k, other], from_core.at[k], core_send, core_recv, k, sibling)

    def chip_copy(k):
        return remote(outgoing.at[k], from_chip.at[k], chip_send, chip_recv, k, across)

    def hid_copy(k):
        return remote(hidden.at[k, core], hidden.at[k, core], hid_send, hid_recv, k, sibling)

    def c_copy(k):
        return remote(result.at[k], returned.at[slots[k]], c_send, c_recv, slots[k], {"ep": peers[k]})

    a_copy(1).start()

    @pl.when(middle == 1)
    def _():
        a_copy(2).start()
        for k in (1, 2):
            pl.semaphore_signal(far_sem.at[0], inc=1, device_id={"ep": peers[k]}, device_id_type=MESH)

    def second_sends():
        a_copy(1).wait_send()
        pl.semaphore_wait(far_sem.at[0], 1)

        @pl.when(middle == 1)
        def _():
            pl.semaphore_signal(far_sem.at[1], inc=1, device_id={"ep": peers[2]}, device_id_type=MESH)

        @pl.when(middle == 0)
        def _():
            a_copy(2).start()

    def third_send(after):
        @pl.when(middle == 0)
        def _():
            if after:
                a_copy(2).wait_send()
            pl.semaphore_wait(far_sem.at[1], 1)
            a_copy(3).start()

        if after:
            @pl.when(middle == 1)
            def _():
                a_copy(2).wait_send()

    half = rows // 2

    scores = scores_ref[...]
    weights = SCALE * scores / jnp.sum(scores, axis=0, keepdims=True)
    routes = routes_ref[...]
    square = (rows, rows)
    diagonal = lax.broadcasted_iota(jnp.int32, square, 0) == lax.broadcasted_iota(jnp.int32, square, 1)
    factors = []
    for k in range(N):
        row = jnp.sum(jnp.where(routes == peers[k], weights, 0.0), axis=0, keepdims=True)
        factors.append(jnp.sum(jnp.where(diagonal, row, 0.0), axis=1, keepdims=True))

    def up_stage(k):
        if k == 0:
            load_tok.wait()
            load_up.wait()
        else:
            a_copy(k).wait_recv()
        if k == 1:
            @pl.when(middle == 1)
            def _():
                forward_copy().start()

        value = jnp.dot(arrived[slots[k]], up[...], preferred_element_type=jnp.float32).astype(jnp.bfloat16)
        part[k] = value.reshape(2, half, value.shape[1])
        core_copy(k).start()

    def chip_stage(k):
        core_copy(k).wait_recv()
        both = part[k, core].astype(jnp.float32) + from_core[k].astype(jnp.float32)
        pair_sum[k] = both
        outgoing[k] = both.astype(jnp.bfloat16)
        chip_copy(k).start()

    def hidden_stage(k):
        chip_copy(k).wait_recv()
        value = pair_sum[k] + from_chip[k].astype(jnp.float32)
        hidden[k, core] = (value / (1.0 + jnp.exp(-value))).astype(jnp.bfloat16)
        hid_copy(k).start()

    def down_stage(k):
        hid_copy(k).wait_recv()
        if k == 1:
            load_down.wait()
        rows_in = hidden[k].reshape(rows, hidden.shape[3])
        value = jnp.dot(rows_in, down[...], preferred_element_type=jnp.float32).astype(jnp.bfloat16)
        if k == 0:
            returned[0] = value
        else:
            result[k] = value
            c_copy(k).start()

    stages = {"u": up_stage, "c": chip_stage, "h": hidden_stage, "d": down_stage}
    for step in SCHEDULE:
        if step == "S2":
            second_sends()
        elif step in ("S3", "X3"):
            third_send(step == "S3")
        else:
            stages[step[0]](int(step[1]))

    mixed = jnp.zeros(out_ref.shape, jnp.float32)
    for k in range(N):
        if k > 0:
            c_copy(k).wait_recv()
        mixed = mixed + factors[k] * returned[slots[k]].astype(jnp.float32)
    out_ref[...] = mixed.astype(out_ref.dtype)

    for k in range(N):
        core_copy(k).wait_send()
        chip_copy(k).wait_send()
        hid_copy(k).wait_send()
        if k > 0:
            if k == 3 or (k == 2 and "X3" in SCHEDULE):
                a_copy(k).wait_send()
            c_copy(k).wait_send()


def dense_body(tokens, routes, scores, w_up, w_down):
    rows, quarter = tokens.shape
    width = w_up.shape[2]
    half = rows // 2
    bf16, f32 = jnp.bfloat16, jnp.float32
    vmem = pl.BlockSpec(memory_space=pltpu.VMEM)
    anywhere = pl.BlockSpec(memory_space=pl.ANY)
    dma = pltpu.SemaphoreType.DMA
    return pl.pallas_call(
        kernel,
        out_shape=jax.ShapeDtypeStruct((rows, quarter), bf16),
        in_specs=[anywhere, vmem, vmem, anywhere, anywhere],
        out_specs=vmem,
        scratch_shapes=[
            pltpu.VMEM((quarter, width), bf16),
            pltpu.VMEM((width, quarter), bf16),
            pltpu.VMEM((N, rows, quarter), bf16),
            pltpu.VMEM((N, 2, half, width), bf16),
            pltpu.VMEM((N, half, width), bf16),
            pltpu.VMEM((N, half, width), bf16),
            pltpu.VMEM((N, half, width), f32),
            pltpu.VMEM((N, half, width), bf16),
            pltpu.VMEM((N, 2, half, width), bf16),
            pltpu.VMEM((N, rows, quarter), bf16),
            pltpu.VMEM((N, rows, quarter), bf16),
            dma((3,)),
        ] + [dma((N,))] * 10 + [pltpu.SemaphoreType.REGULAR((2,))],
        compiler_params=pltpu.CompilerParams(
            collective_id=0, has_side_effects=True, vmem_limit_bytes=60 * 1024 * 1024
        ),
        cost_estimate=pl.CostEstimate(
            flops=4 * N * rows * quarter * width, bytes_accessed=4 * quarter * width, transcendentals=N * rows * width
        ),
        name="expert_layer",
    )(tokens, routes.T, scores.T, w_up, w_down)


def body(tokens, routes, scores, w_up, w_down):
    rows_here, quarter = tokens.shape
    chosen = routes.shape[1]
    owners = lax.axis_size("ep")
    capacity = 2 * rows_here * chosen // owners
    flat_ids = routes.reshape(-1)
    onehot = (flat_ids[:, None] == jnp.arange(owners, dtype=jnp.int32)[None, :]).astype(jnp.int32)
    slot_rank = jnp.sum((jnp.cumsum(onehot, axis=0) - onehot) * onehot, axis=1)
    target = flat_ids * capacity + slot_rank
    pair_token = jnp.arange(rows_here * chosen, dtype=jnp.int32) // chosen
    matches = target[None, :] == jnp.arange(owners * capacity, dtype=jnp.int32)[:, None]
    source = jnp.sum(jnp.where(matches, pair_token[None, :] + 1, 0), axis=1) - 1
    picked = jnp.take(tokens, jnp.maximum(source, 0), axis=0)
    outgoing = jnp.where((source >= 0)[:, None], picked, jnp.zeros_like(picked)).reshape(
        owners, capacity, quarter
    )
    up_local = w_up[0]
    down_local = w_down[0]
    arrived = lax.all_to_all(outgoing, "ep", split_axis=0, concat_axis=0, tiled=True)
    senders, slot_count, columns = arrived.shape
    flat_rows = arrived.reshape(senders * slot_count, columns)
    partial_value = jnp.dot(flat_rows, up_local, preferred_element_type=jnp.float32)
    hidden = jax.nn.silu(
        lax.psum(partial_value.astype(jnp.bfloat16), "tp").astype(jnp.float32)
    ).astype(jnp.bfloat16)
    result = jnp.dot(hidden, down_local, preferred_element_type=jnp.float32).astype(jnp.bfloat16)
    returned_rows = lax.all_to_all(
        result.reshape(senders, slot_count, columns), "ep", split_axis=0, concat_axis=0, tiled=True
    )
    back_flat = returned_rows.reshape(owners * capacity, quarter)
    gathered = (
        jnp.take(back_flat, target, axis=0).reshape(rows_here, chosen, quarter).astype(jnp.float32)
    )
    weights = SCALE * scores / jnp.sum(scores, axis=1, keepdims=True)
    mixed = jnp.einsum("tk,tkd->td", weights, gathered, precision=lax.Precision.HIGHEST)
    return mixed.astype(jnp.bfloat16)


def solution(mesh):
    in_specs = (
        P(("group", "ep"), "tp"),
        P(("group", "ep"), None),
        P(("group", "ep"), None),
        P("ep", "tp", None),
        P("ep", None, "tp"),
    )
    out_specs = P(("group", "ep"), "tp")
    shape = mesh.shape
    small = shape["ep"] == N and shape["tp"] == N
    return jax.shard_map(dense_body if small else body, mesh=mesh, in_specs=in_specs, out_specs=out_specs, check_vma=False)
```
